256 devices in a mesh: head: 32 (over x, z_lo, core), ctx: 8 (over y, z_hi).
Axes of the slice: x: 4, y: 4, z: 8 (z_hi: 2, z_lo: 4; z = z_hi * 4 + z_lo), core: 2. Of those that a mesh axis runs over, the one named last changes fastest.
Arguments:
- queries: bfloat16 [32768, 8192], P('ctx', 'head'), may hold values from -6 to 6
- keys: bfloat16 [1024, 512], P(('head', 'ctx')), may hold values from -6 to 6
- values: bfloat16 [1024, 512], P(('head', 'ctx')), may hold values from -6 to 6
- outputs: bfloat16 [32768, 8192], P('ctx', 'head'), may hold values from -6 to 6
- dout: bfloat16 [32768, 8192], P(('ctx', 'head')), may hold values from -24 to 24
- lse: float32 [64, 32768], P('head', 'ctx'), may hold values from 6.5 to 8.5
Outputs:
- dq: bfloat16 [32768, 8192], P('ctx', 'head')
- dk: bfloat16 [1024, 512], P(('head', 'ctx'))
- dv: bfloat16 [1024, 512], P(('head', 'ctx'))
The draws below stay inside these ranges and needn't reach their ends.
All inputs are finite; a program needn't handle non-finite values.
Results may differ from the reference program's by a relative error of at most 0.0052.
Values may be sent and summed in bfloat16 or wider, within the bound.
A program may use at most 128 MiB of HBM per device.

```python
import jax
import jax.numpy as jnp
from jax import lax

QUERY_HEADS = 64
KEY_VALUE_HEADS = 4
HEAD_SIZE = 128
SQ = 32768
TOTAL_KEYS = 1024


def steps_of(stream_key, dims, split, least, top_value):
    def one(dim, parts):
        heights = jax.random.uniform(jax.random.fold_in(jax.random.fold_in(stream_key, 6), dim), (parts,), jnp.float32, least / len(split), top_value / len(split))
        return jnp.repeat(jnp.exp(heights), dims[dim] // parts).reshape((-1,) + (1,) * (len(dims) - dim - 1))

    level = one(*split[0])
    for cut in split[1:]:
        level = level * one(*cut)
    return level


def scatter_about(key, extent, spread, reach, shards=(), kind=jnp.bfloat16):
    values = spread * jax.random.normal(key, extent, jnp.float32)
    if shards:
        values = values * steps_of(key, extent, shards, -0.22, 0.18)
    return jnp.clip(values, -reach, reach).astype(kind)


def setup_inputs(seed: int = 0) -> dict:
    key_of = jax.random.split(jax.random.key(seed), 7)
    return {
        "queries": scatter_about(key_of[0], (SQ, QUERY_HEADS * HEAD_SIZE), 1.0, 6.0, ((0, 8), (1, 32))),
        "keys": scatter_about(key_of[1], (TOTAL_KEYS, KEY_VALUE_HEADS * HEAD_SIZE), 1.0, 6.0, ((0, 256),)),
        "values": scatter_about(key_of[2], (TOTAL_KEYS, KEY_VALUE_HEADS * HEAD_SIZE), 1.0, 6.0, ((0, 256),)),
        "outputs": scatter_about(key_of[3], (SQ, QUERY_HEADS * HEAD_SIZE), 1.0, 6.0, ((0, 8), (1, 32))),
        "dout": scatter_about(key_of[4], (SQ, QUERY_HEADS * HEAD_SIZE), 4.0, 24.0, ((0, 256),)),
        "lse": jnp.clip(6.5 + 2.0 * jax.random.uniform(key_of[5], (QUERY_HEADS, SQ), jnp.float32) ** steps_of(key_of[5], (QUERY_HEADS, SQ), ((0, 32), (1, 8)), -0.2, 0.2), 6.5, 8.5),
    }


def reference(queries, keys, values, outputs, dout, lse):
    factor = HEAD_SIZE ** -0.5
    heads_per_group = QUERY_HEADS // KEY_VALUE_HEADS
    dq_parts = []
    dk_parts = []
    dv_parts = []
    for key_value_index in range(KEY_VALUE_HEADS):
        key_group = keys[:, key_value_index * HEAD_SIZE:(key_value_index + 1) * HEAD_SIZE]
        value_group = values[:, key_value_index * HEAD_SIZE:(key_value_index + 1) * HEAD_SIZE]
        first = key_value_index * heads_per_group
        span = slice(first * HEAD_SIZE, (first + heads_per_group) * HEAD_SIZE)
        q_stack = queries[:, span].reshape(SQ, heads_per_group, HEAD_SIZE).transpose(1, 0, 2)
        o_stack = outputs[:, span].reshape(SQ, heads_per_group, HEAD_SIZE).transpose(1, 0, 2)
        d_stack = dout[:, span].reshape(SQ, heads_per_group, HEAD_SIZE).transpose(1, 0, 2)
        l_stack = lse[first:first + heads_per_group]

        def one_head(carry, items):
            q_head, o_head, d_head, l_head = items
            scores = jnp.dot(q_head, key_group.T, preferred_element_type=jnp.float32) * factor
            probs = jnp.exp(scores - l_head[:, None])
            probs_low = probs.astype(jnp.bfloat16)
            dv_term = jnp.dot(probs_low.T, d_head, preferred_element_type=jnp.float32)
            dprobs = jnp.dot(d_head, value_group.T, preferred_element_type=jnp.float32)
            delta = jnp.sum(d_head.astype(jnp.float32) * o_head.astype(jnp.float32), axis=1)
            dscores = (probs * (dprobs - delta[:, None])).astype(jnp.bfloat16)
            dq_head = (jnp.dot(dscores, key_group, preferred_element_type=jnp.float32) * factor).astype(jnp.bfloat16)
            dk_term = jnp.dot(dscores.T, q_head, preferred_element_type=jnp.float32)
            return (carry[0] + dk_term, carry[1] + dv_term), dq_head

        zero_filled = jnp.zeros((TOTAL_KEYS, HEAD_SIZE), jnp.float32)
        (dk_sum, dv_sum), dq_stack = lax.scan(one_head, (zero_filled, zero_filled), (q_stack, o_stack, d_stack, l_stack))
        dq_parts.append(dq_stack.transpose(1, 0, 2).reshape(SQ, heads_per_group * HEAD_SIZE))
        dk_parts.append((dk_sum * factor).astype(jnp.bfloat16))
        dv_parts.append(dv_sum.astype(jnp.bfloat16))
    return (jnp.concatenate(dq_parts, axis=1), jnp.concatenate(dk_parts, axis=1), jnp.concatenate(dv_parts, axis=1))
```

```python
import functools
import math

import jax
import jax.numpy as jnp
from jax import lax
from jax.experimental import pallas as pl
from jax.experimental.pallas import tpu as pltpu
from jax.sharding import PartitionSpec as P

MESH = pl.DeviceIdType.MESH
D = 128
T = 128
NX, NZL, NC, NY, NZH = 4, 4, 2, 4, 2
NZ = NZL * NZH
NH = NX * NZL * NC
KEYS = 1024
GROUP = 16
KB = 256
C = D ** (-0.5)
LOG2E = math.log2(math.e)
NT = (((1,), (1,)), ((), ()))
F32, BF16 = jnp.float32, jnp.bfloat16


def div(a, n):
    return lax.div(a, jnp.int32(n))


def rem(a, n):
    return lax.rem(a, jnp.int32(n))


def kernel(
    q_hbm, k_ref, v_ref, o_hbm, d_hbm, lse_ref,
    dq_hbm, dk_ref, dv_ref,
    q_vm, o_vm, d_vm, dq_vm,
    a_out, a_in, kv16, kv, kk, vv, kt,
    acc, rd_in, rc_out, rc_in, tot, rb_out, rb_in, last, ra_out, ra_in,
    d_send, d_recv, q_sem, o_sem, dq_sem,
    ka_send, ka_recv, kb_send, kb_recv, kc_send, kc_recv, kd_send, kd_recv,
    rd_send, rd_recv, rc_send, rc_recv, rb_send, rb_recv, ra_send, ra_recv,
):
    head, ctx = lax.axis_index("head"), lax.axis_index("ctx")
    x, zl, core = div(head, NZL * NC), rem(div(head, NC), NZL), rem(head, NC)
    y, zh = div(ctx, NZH), rem(ctx, NZH)
    z = zh * NZL + zl
    za, zb = div(zl, 2), rem(zl, 2)

    def device(x_=x, zl_=zl, core_=core, y_=y, zh_=zh):
        return ((x_ * NZL + zl_) * NC + core_, y_ * NZH + zh_)

    def partner(j, way):
        da, dc, db, dx = rem(j, 2), rem(div(j, 2), 2), rem(div(j, 4), 2), div(j, 8)
        x_ = rem(x + NX + way * dx, NX)
        zl_ = rem(za + da, 2) * 2 + rem(zb + db, 2)
        return (x_ * NZL + zl_) * NC + rem(core + dc, NC)

    q_copy = pltpu.make_async_copy(q_hbm, q_vm, q_sem)
    o_copy = pltpu.make_async_copy(o_hbm, o_vm, o_sem)
    own = pltpu.make_async_copy(
        d_hbm.at[:, pl.ds(pl.multiple_of(head * 2 * D, 2 * D), 2 * D)], d_vm.at[head], d_recv.at[0]
    )

    barrier = pltpu.get_barrier_semaphore()

    @pl.loop(1, NH)
    def _(j):
        pl.semaphore_signal(barrier, inc=1, device_id=(partner(j, 1), ctx), device_id_type=MESH)

    for r in range(1, NY):
        pl.semaphore_signal(barrier, inc=1, device_id=device(y_=rem(y + r, NY)), device_id_type=MESH)
    for r in range(NZL):
        pl.semaphore_signal(
            barrier, inc=1, device_id=device(zl_=rem(zl + r, NZL), zh_=1 - zh), device_id_type=MESH
        )
    own.start()
    q_copy.start()
    o_copy.start()
    for g in range(NX):
        a_out[g, 0:4, :] = k_ref[:, g * D : (g + 1) * D].astype(F32)
        a_out[g, 4:8, :] = v_ref[:, g * D : (g + 1) * D].astype(F32)
    pl.semaphore_wait(barrier, NH - 1 + NY - 1 + NZL)

    def exchange(n, me, target, src, dst, send, recv):
        copies = []
        for r in range(1, n):
            to = rem(me + r, n)
            copy = pltpu.make_async_remote_copy(
                src_ref=src(to), dst_ref=dst(me), send_sem=send.at[r], recv_sem=recv.at[r],
                device_id=target(to), device_id_type=MESH,
            )
            copy.start()
            copies.append(copy)
        return copies

    ka = exchange(NX, x, lambda i: device(x_=i), lambda i: a_out.at[i], lambda i: a_in.at[i], ka_send, ka_recv)

    def block_copy(j):
        to = partner(j, 1)
        return pltpu.make_async_remote_copy(
            src_ref=d_hbm.at[:, pl.ds(pl.multiple_of(to * 2 * D, 2 * D), 2 * D)],
            dst_ref=d_vm.at[head],
            send_sem=d_send.at[j], recv_sem=d_recv.at[j],
            device_id=(to, ctx), device_id_type=MESH,
        )

    @pl.loop(1, NH)
    def _(j):
        block_copy(j).start()

    a_in[x] = a_out[x]
    for copy in ka:
        copy.wait()
    for p in range(NX):
        kv16[0, 4 * p : 4 * p + 4, :] = a_in[p, 0:4, :]
        kv16[1, 4 * p : 4 * p + 4, :] = a_in[p, 4:8, :]
    kv[core, y, z] = kv16[...].astype(BF16)

    def zdev(i):
        return device(zl_=rem(i, NZL), zh_=div(i, NZL))

    kb = exchange(NZ, z, zdev, lambda i: kv.at[core, y, z], lambda i: kv.at[core, y, i], kb_send, kb_recv)
    acc[...] = jnp.zeros_like(acc)
    for copy in kb:
        copy.wait()
    kc = exchange(NY, y, lambda i: device(y_=i), lambda i: kv.at[core, y], lambda i: kv.at[core, i], kc_send, kc_recv)
    for copy in kc:
        copy.wait()
    kd = exchange(NC, core, lambda i: device(core_=i), lambda i: kv.at[core], lambda i: kv.at[i], kd_send, kd_recv)
    for copy in kd:
        copy.wait()
    for i in range(NC * NY):
        rows = slice(i * 128, (i + 1) * 128)
        kk[rows, :] = kv[i // NY, i % NY, :, 0].reshape(128, D)
        vv[rows, :] = kv[i // NY, i % NY, :, 1].reshape(128, D)
    for i in range(KEYS // KB):
        kt[:, i * KB : (i + 1) * KB] = kk[i * KB : (i + 1) * KB, :].T
    q_copy.wait()
    o_copy.wait()

    def stack(block):
        return jnp.concatenate([block[:, :D], block[:, D:]], axis=0)

    @pl.loop(0, NH)
    def _(t):
        j = rem(t, NH // 2) * 2 + div(t, NH // 2)
        src = partner(j, -1)
        pltpu.make_async_copy(d_vm.at[src], d_vm.at[src], d_recv.at[j]).wait()
        rows = pl.ds(pl.multiple_of(src * T, T), T)
        q = stack(q_vm[rows, :])
        d = stack(d_vm[src])
        o = stack(o_vm[rows, :])
        delta = jnp.sum((d.astype(F32) * o.astype(F32)).T, axis=0, keepdims=True)
        lse = lse_ref[:, rows] * LOG2E
        lse = jnp.concatenate([lse[0:1], lse[1:2]], axis=1)
        dqt = jnp.zeros((D, 2 * T), F32)
        for i in range(KEYS // KB):
            at = slice(i * KB, (i + 1) * KB)
            s = lax.dot_general(kk[at, :], q, NT, preferred_element_type=F32)
            p = jnp.exp2(s * (C * LOG2E) - lse)
            dp = lax.dot_general(vv[at, :], d, NT, preferred_element_type=F32)
            ds = (p * (dp - delta)).astype(BF16)
            acc[1, at, :] += jnp.dot(p.astype(BF16), d, preferred_element_type=F32)
            acc[0, at, :] += jnp.dot(ds, q, preferred_element_type=F32)
            dqt = dqt + jnp.dot(kt[:, at], ds, preferred_element_type=F32)
        dq = (dqt * C).T.astype(BF16)
        dq_vm[rows, 0:D] = dq[0:T]
        dq_vm[rows, D : 2 * D] = dq[T : 2 * T]
        pltpu.make_async_copy(dq_vm.at[rows, :], dq_hbm.at[rows, :], dq_sem.at[j]).start()

    half = KEYS // NC
    part = half // NY
    rd = []
    for i in range(2):
        copy = pltpu.make_async_remote_copy(
            src_ref=acc.at[i, pl.ds(pl.multiple_of((1 - core) * half, half), half)],
            dst_ref=rd_in.at[i], send_sem=rd_send.at[i], recv_sem=rd_recv.at[i],
            device_id=device(core_=1 - core), device_id_type=MESH,
        )
        copy.start()
        rd.append(copy)

    def halves(i, yy):
        mine = pl.ds(pl.multiple_of(core * half + yy * part, part), part)
        return acc[i, mine, :] + rd_in[i, pl.ds(pl.multiple_of(yy * part, part), part), :]

    for i in range(2):
        rd[i].wait()
    for r in range(1, NY):
        to = rem(y + r, NY)
        for i in range(2):
            rc_out[to, i] = halves(i, to).astype(rc_out.dtype)
    rc = exchange(NY, y, lambda i: device(y_=i), lambda i: rc_out.at[i], lambda i: rc_in.at[i], rc_send, rc_recv)
    for i in range(2):
        tot[i] = halves(i, y)
    for r in range(1, NY):
        rc[r - 1].wait()
        tot[...] += rc_in[rem(y + NY - r, NY)].astype(F32)
    for zz in range(NZ):
        rb_out[zz] = tot[:, zz * GROUP : (zz + 1) * GROUP, :].astype(rb_out.dtype)
    rb = exchange(NZ, z, zdev, lambda i: rb_out.at[i], lambda i: rb_in.at[i], rb_send, rb_recv)
    last[...] = tot[:, pl.ds(pl.multiple_of(z * GROUP, GROUP), GROUP), :]
    for r in range(1, NZ):
        rb[r - 1].wait()
        last[...] += rb_in[rem(z + NZ - r, NZ)].astype(F32)
    for p in range(NX):
        ra_out[p, 0:4, :] = last[0, 4 * p : 4 * p + 4, :] * C
        ra_out[p, 4:8, :] = last[1, 4 * p : 4 * p + 4, :]
    ra = exchange(NX, x, lambda i: device(x_=i), lambda i: ra_out.at[i], lambda i: ra_in.at[i], ra_send, ra_recv)
    ra_in[x] = ra_out[x]

    @pl.loop(0, NH)
    def _(j):
        rows = pl.ds(pl.multiple_of(partner(j, -1) * T, T), T)
        pltpu.make_async_copy(dq_vm.at[rows, :], dq_hbm.at[rows, :], dq_sem.at[j]).wait()

    @pl.loop(1, NH)
    def _(j):
        block_copy(j).wait_send()

    for copy in ra:
        copy.wait()
    for g in range(NX):
        dk_ref[:, g * D : (g + 1) * D] = ra_in[g, 0:4, :].astype(BF16)
        dv_ref[:, g * D : (g + 1) * D] = ra_in[g, 4:8, :].astype(BF16)


def on_device(queries, keys, values, outputs, dout, lse):
    tokens = queries.shape[0]
    wire = F32
    dma = pltpu.SemaphoreType.DMA
    part = KEYS // NC // NY
    hbm = pl.BlockSpec(memory_space=pltpu.HBM)
    vmem = pl.BlockSpec(memory_space=pltpu.VMEM)
    flops = 5 * 2 * 2 * tokens * KEYS * D
    return pl.pallas_call(
        kernel,
        out_shape=(
            jax.ShapeDtypeStruct((tokens, 2 * D), BF16),
            jax.ShapeDtypeStruct(keys.shape, BF16),
            jax.ShapeDtypeStruct(values.shape, BF16),
        ),
        in_specs=[hbm, vmem, vmem, hbm, hbm, vmem],
        out_specs=(hbm, vmem, vmem),
        scratch_shapes=[
            pltpu.VMEM((tokens, 2 * D), BF16),
            pltpu.VMEM((tokens, 2 * D), BF16),
            pltpu.VMEM((NH, T, 2 * D), BF16),
            pltpu.VMEM((tokens, 2 * D), BF16),
            pltpu.VMEM((NX, 8, D), F32),
            pltpu.VMEM((NX, 8, D), F32),
            pltpu.VMEM((2, GROUP, D), F32),
            pltpu.VMEM((NC, NY, NZ, 2, GROUP, D), BF16),
            pltpu.VMEM((KEYS, D), BF16),
            pltpu.VMEM((KEYS, D), BF16),
            pltpu.VMEM((D, KEYS), BF16),
            pltpu.VMEM((2, KEYS, D), F32),
            pltpu.VMEM((2, KEYS // NC, D), F32),
            pltpu.VMEM((NY, 2, part, D), wire),
            pltpu.VMEM((NY, 2, part, D), wire),
            pltpu.VMEM((2, part, D), F32),
            pltpu.VMEM((NZ, 2, GROUP, D), wire),
            pltpu.VMEM((NZ, 2, GROUP, D), wire),
            pltpu.VMEM((2, GROUP, D), F32),
            pltpu.VMEM((NX, 8, D), F32),
            pltpu.VMEM((NX, 8, D), F32),
            dma((NH,)), dma((NH,)), dma, dma, dma((NH,)),
            dma((NX,)), dma((NX,)), dma((NZ,)), dma((NZ,)), dma((NY,)), dma((NY,)), dma((NC,)), dma((NC,)),
            dma((2,)), dma((2,)), dma((NY,)), dma((NY,)), dma((NZ,)), dma((NZ,)), dma((NX,)), dma((NX,)),
        ],
        compiler_params=pltpu.CompilerParams(
            collective_id=0, has_side_effects=True, vmem_limit_bytes=56 * 1024 * 1024
        ),
        cost_estimate=pl.CostEstimate(
            flops=flops, bytes_accessed=8 * tokens * 2 * D, transcendentals=2 * tokens * KEYS
        ),
        name="attention_backward",
    )(queries, keys, values, outputs, dout, lse)


def solution(mesh):
    placed = (
        P("ctx", "head"),
        P(("head", "ctx"), None),
        P(("head", "ctx"), None),
        P("ctx", "head"),
        P(("ctx", "head"), None),
        P("head", "ctx"),
    )
    return jax.shard_map(
        on_device,
        mesh=mesh,
        in_specs=placed,
        out_specs=(P("ctx", "head"), P(("head", "ctx"), None), P(("head", "ctx"), None)),
        check_vma=False,
    )
```

```python
import functools
import math

import jax
import jax.numpy as jnp
from jax import lax
from jax.experimental import pallas as pl
from jax.experimental.pallas import tpu as pltpu
from jax.sharding import PartitionSpec as P

MESH = pl.DeviceIdType.MESH
D = 128
T = 128
NX, NZL, NC, NY, NZH = 4, 4, 2, 4, 2
NZ = NZL * NZH
NH = NX * NZL * NC
KEYS = 1024
GROUP = 16
KB = 256
PACE = (6, 6, 8)
FINISH = 8
C = D ** (-0.5)
LOG2E = math.log2(math.e)
NT = (((1,), (1,)), ((), ()))
F32, BF16 = jnp.float32, jnp.bfloat16


def div(a, n):
    return lax.div(a, jnp.int32(n))


def rem(a, n):
    return lax.rem(a, jnp.int32(n))


def kernel(
    q_hbm, k_ref, v_ref, o_hbm, d_hbm, lse_ref,
    dq_vm, ra_in,
    q_vm, o_vm, d_vm,
    a_out, a_in, kv16, kv, kk, vv, kt,
    acc, rd_in, rc_out, rc_in, tot, rb_out, rb_in, last, ra_out,
    d_send, d_recv, q_sem, o_sem,
    ka_send, ka_recv, kb_send, kb_recv, kc_send, kc_recv, kd_send, kd_recv,
    rd_send, rd_recv, rc_send, rc_recv, rb_send, rb_recv, ra_send, ra_recv,
):
    head, ctx = lax.axis_index("head"), lax.axis_index("ctx")
    x, zl, core = div(head, NZL * NC), rem(div(head, NC), NZL), rem(head, NC)
    y, zh = div(ctx, NZH), rem(ctx, NZH)
    z = zh * NZL + zl
    za, zb = div(zl, 2), rem(zl, 2)

    def device(x_=x, zl_=zl, core_=core, y_=y, zh_=zh):
        return ((x_ * NZL + zl_) * NC + core_, y_ * NZH + zh_)

    def partner(j, way):
        da, dx, dc, db = rem(j, 2), rem(div(j, 2), NX), rem(div(j, 2 * NX), 2), div(j, 4 * NX)
        core_ = rem(core + dc, NC)
        turn = way * (1 - 2 * (core if way == 1 else core_))
        x_ = rem(x + NX + turn * dx, NX)
        zl_ = rem(za + da, 2) * 2 + rem(zb + db, 2)
        return (x_ * NZL + zl_) * NC + core_

    q_copy = pltpu.make_async_copy(q_hbm, q_vm, q_sem)
    o_copy = pltpu.make_async_copy(o_hbm, o_vm, o_sem)
    own = pltpu.make_async_copy(
        d_hbm.at[:, pl.ds(pl.multiple_of(head * 2 * D, 2 * D), 2 * D)], d_vm.at[head], d_recv.at[0]
    )

    barrier = pltpu.get_barrier_semaphore()

    @pl.loop(1, NH)
    def _(j):
        pl.semaphore_signal(barrier, inc=1, device_id=(partner(j, 1), ctx), device_id_type=MESH)

    for r in range(1, NY):
        pl.semaphore_signal(barrier, inc=1, device_id=device(y_=rem(y + r, NY)), device_id_type=MESH)
    for r in range(NZL):
        pl.semaphore_signal(
            barrier, inc=1, device_id=device(zl_=rem(zl + r, NZL), zh_=1 - zh), device_id_type=MESH
        )
    for g in range(NX):
        a_out[g, 0:4, :] = k_ref[:, g * D : (g + 1) * D].astype(F32)
        a_out[g, 4:8, :] = v_ref[:, g * D : (g + 1) * D].astype(F32)
    pl.semaphore_wait(barrier, NH - 1 + NY - 1 + NZL)

    def exchange(n, me, target, src, dst, send, recv):
        copies = []
        for r in range(1, n):
            to = rem(me + r, n)
            copy = pltpu.make_async_remote_copy(
                src_ref=src(to), dst_ref=dst(me), send_sem=send.at[r], recv_sem=recv.at[r],
                device_id=target(to), device_id_type=MESH,
            )
            copy.start()
            copies.append(copy)
        return copies

    ka = exchange(NX, x, lambda i: device(x_=i), lambda i: a_out.at[i], lambda i: a_in.at[i], ka_send, ka_recv)

    def block_copy(j):
        to = partner(j, 1)
        return pltpu.make_async_remote_copy(
            src_ref=d_hbm.at[:, pl.ds(pl.multiple_of(to * 2 * D, 2 * D), 2 * D)],
            dst_ref=d_vm.at[head],
            send_sem=d_send.at[j], recv_sem=d_recv.at[j],
            device_id=(to, ctx), device_id_type=MESH,
        )

    def start_blocks(first, end):
        @pl.loop(first, end)
        def _(j):
            block_copy(j).start()

    start_blocks(1, 1 + PACE[0])
    a_in[x] = a_out[x]
    for copy in ka:
        copy.wait()
    for p in range(NX):
        kv16[0, 4 * p : 4 * p + 4, :] = a_in[p, 0:4, :]
        kv16[1, 4 * p : 4 * p + 4, :] = a_in[p, 4:8, :]
    kv[core, y, z] = kv16[...].astype(BF16)

    def zdev(i):
        return device(zl_=rem(i, NZL), zh_=div(i, NZL))

    kb = exchange(NZ, z, zdev, lambda i: kv.at[core, y, z], lambda i: kv.at[core, y, i], kb_send, kb_recv)
    start_blocks(1 + PACE[0], 1 + PACE[0] + PACE[1])
    own.start()
    q_copy.start()
    o_copy.start()
    acc[...] = jnp.zeros_like(acc)
    for copy in kb:
        copy.wait()
    kc = exchange(NY, y, lambda i: device(y_=i), lambda i: kv.at[core, y], lambda i: kv.at[core, i], kc_send, kc_recv)

    def sibling(r):
        at = rem(y + NY - r, NY)
        return pltpu.make_async_remote_copy(
            src_ref=kv.at[core, at], dst_ref=kv.at[core, at], send_sem=kd_send.at[r], recv_sem=kd_recv.at[r],
            device_id=device(core_=1 - core), device_id_type=MESH,
        )

    sibling(0).start()
    start_blocks(1 + PACE[0] + PACE[1], 1 + sum(PACE))
    for r in range(1, NY):
        kc[r - 1].wait()
        sibling(r).start()
    for r in range(NY):
        sibling(r).wait()
    for i in range(NC * NY):
        rows = slice(i * 128, (i + 1) * 128)
        kk[rows, :] = kv[i // NY, i % NY, :, 0].reshape(128, D)
        vv[rows, :] = kv[i // NY, i % NY, :, 1].reshape(128, D)
    for i in range(KEYS // KB):
        kt[:, i * KB : (i + 1) * KB] = kk[i * KB : (i + 1) * KB, :].T
    q_copy.wait()
    o_copy.wait()

    def stack(block):
        return jnp.concatenate([block[:, :D], block[:, D:]], axis=0)

    def arrived(j):
        src = partner(j, -1)
        pltpu.make_async_copy(d_vm.at[src], d_vm.at[src], d_recv.at[j]).wait()
        return src

    @pl.loop(0, NH, step=2)
    def _(j):
        for i in range(2):
            ahead = 1 + sum(PACE) + j + i

            @pl.when(ahead < NH)
            def _():
                block_copy(ahead).start()

        pair = [arrived(j), arrived(j + 1)]
        rows = [pl.ds(pl.multiple_of(src * T, T), T) for src in pair]
        q = jnp.concatenate([stack(q_vm[at, :]) for at in rows], axis=0)
        d = jnp.concatenate([stack(d_vm[src]) for src in pair], axis=0)
        o = jnp.concatenate([stack(o_vm[at, :]) for at in rows], axis=0)
        delta = jnp.sum((d.astype(F32) * o.astype(F32)).T, axis=0, keepdims=True)
        lse = [lse_ref[:, at] * LOG2E for at in rows]
        lse = jnp.concatenate([row for pairs in lse for row in (pairs[0:1], pairs[1:2])], axis=1)
        dqt = jnp.zeros((D, 4 * T), F32)
        for i in range(KEYS // KB):
            at = slice(i * KB, (i + 1) * KB)
            s = lax.dot_general(kk[at, :], q, NT, preferred_element_type=F32)
            p = jnp.exp2(s * (C * LOG2E) - lse)
            dp = lax.dot_general(vv[at, :], d, NT, preferred_element_type=F32)
            ds = (p * (dp - delta)).astype(BF16)
            acc[1, at, :] += jnp.dot(p.astype(BF16), d, preferred_element_type=F32)
            acc[0, at, :] += jnp.dot(ds, q, preferred_element_type=F32)
            dqt = dqt + jnp.dot(kt[:, at], ds, preferred_element_type=F32)
        dq = (dqt * C).T.astype(BF16)
        for i in range(2):
            dq_vm[rows[i], 0:D] = dq[2 * i * T : (2 * i + 1) * T]
            dq_vm[rows[i], D : 2 * D] = dq[(2 * i + 1) * T : (2 * i + 2) * T]

    half = KEYS // NC
    part = half // NY
    rd = []
    for r in (1, 2, 3, 0):
        to = rem(y + r, NY)
        copy = pltpu.make_async_remote_copy(
            src_ref=acc.at[:, pl.ds(pl.multiple_of((1 - core) * half + to * part, part), part), :],
            dst_ref=rd_in.at[to], send_sem=rd_send.at[r], recv_sem=rd_recv.at[r],
            device_id=device(core_=1 - core), device_id_type=MESH,
        )
        copy.start()
        rd.append(copy)

    def both(yy):
        return acc[:, pl.ds(pl.multiple_of(core * half + yy * part, part), part), :] + rd_in[yy]

    rc = []
    for r in range(1, NY):
        to = rem(y + r, NY)
        rd[r - 1].wait_recv()
        rc_out[to] = both(to).astype(rc_out.dtype)
        copy = pltpu.make_async_remote_copy(
            src_ref=rc_out.at[to], dst_ref=rc_in.at[y], send_sem=rc_send.at[r], recv_sem=rc_recv.at[r],
            device_id=device(y_=to), device_id_type=MESH,
        )
        copy.start()
        rc.append(copy)
    rd[NY - 1].wait_recv()
    tot[...] = both(y)
    for r in range(1, NY):
        rc[r - 1].wait_recv()
        tot[...] += rc_in[rem(y + NY - r, NY)].astype(F32)
    for zz in range(NZ):
        rb_out[zz] = tot[:, zz * GROUP : (zz + 1) * GROUP, :].astype(rb_out.dtype)
    rb = exchange(NZ, z, zdev, lambda i: rb_out.at[i], lambda i: rb_in.at[i], rb_send, rb_recv)
    last[...] = tot[:, pl.ds(pl.multiple_of(z * GROUP, GROUP), GROUP), :]
    for r in range(1, NZ):
        rb[r - 1].wait_recv()
        last[...] += rb_in[rem(z + NZ - r, NZ)].astype(F32)
    for p in range(NX):
        ra_out[p, 0:4, :] = last[0, 4 * p : 4 * p + 4, :] * C
        ra_out[p, 4:8, :] = last[1, 4 * p : 4 * p + 4, :]
    ra = exchange(NX, x, lambda i: device(x_=i), lambda i: ra_out.at[i], lambda i: ra_in.at[i], ra_send, ra_recv)
    ra_in[x] = ra_out[x]

    @pl.loop(1, NH)
    def _(j):
        block_copy(j).wait_send()

    for copy in rd + rc + rb:
        copy.wait_send()
    for copy in ra:
        copy.wait()


def finish(dq_in, terms, dq_hbm, dk_ref, dv_ref, sem):
    rows = dq_in.shape[0] // FINISH
    copies = [
        pltpu.make_async_copy(dq_in.at[i * rows : (i + 1) * rows], dq_hbm.at[i * rows : (i + 1) * rows], sem.at[i])
        for i in range(FINISH)
    ]
    for copy in copies:
        copy.start()
    for g in range(NX):
        dk_ref[:, g * D : (g + 1) * D] = terms[g, 0:4, :].astype(BF16)
        dv_ref[:, g * D : (g + 1) * D] = terms[g, 4:8, :].astype(BF16)
    for copy in copies:
        copy.wait()


def on_device(queries, keys, values, outputs, dout, lse):
    tokens = queries.shape[0]
    wire = BF16
    dma = pltpu.SemaphoreType.DMA
    part = KEYS // NC // NY
    hbm = pl.BlockSpec(memory_space=pltpu.HBM)
    vmem = pl.BlockSpec(memory_space=pltpu.VMEM)
    flops = 5 * 2 * 2 * tokens * KEYS * D
    dq, terms = pl.pallas_call(
        kernel,
        out_shape=(
            pltpu.VMEM((tokens, 2 * D), BF16),
            jax.ShapeDtypeStruct((NX, 8, D), F32),
        ),
        in_specs=[hbm, vmem, vmem, hbm, hbm, vmem],
        out_specs=(vmem, vmem),
        scratch_shapes=[
            pltpu.VMEM((tokens, 2 * D), BF16),
            pltpu.VMEM((tokens, 2 * D), BF16),
            pltpu.VMEM((NH, T, 2 * D), BF16),
            pltpu.VMEM((NX, 8, D), F32),
            pltpu.VMEM((NX, 8, D), F32),
            pltpu.VMEM((2, GROUP, D), F32),
            pltpu.VMEM((NC, NY, NZ, 2, GROUP, D), BF16),
            pltpu.VMEM((KEYS, D), BF16),
            pltpu.VMEM((KEYS, D), BF16),
            pltpu.VMEM((D, KEYS), BF16),
            pltpu.VMEM((2, KEYS, D), F32),
            pltpu.VMEM((NY, 2, part, D), F32),
            pltpu.VMEM((NY, 2, part, D), wire),
            pltpu.VMEM((NY, 2, part, D), wire),
            pltpu.VMEM((2, part, D), F32),
            pltpu.VMEM((NZ, 2, GROUP, D), wire),
            pltpu.VMEM((NZ, 2, GROUP, D), wire),
            pltpu.VMEM((2, GROUP, D), F32),
            pltpu.VMEM((NX, 8, D), F32),
            dma((NH,)), dma((NH,)), dma, dma,
            dma((NX,)), dma((NX,)), dma((NZ,)), dma((NZ,)), dma((NY,)), dma((NY,)), dma((NY,)), dma((NY,)),
            dma((NY,)), dma((NY,)), dma((NY,)), dma((NY,)), dma((NZ,)), dma((NZ,)), dma((NX,)), dma((NX,)),
        ],
        compiler_params=pltpu.CompilerParams(
            collective_id=0, has_side_effects=True, vmem_limit_bytes=56 * 1024 * 1024
        ),
        cost_estimate=pl.CostEstimate(
            flops=flops, bytes_accessed=8 * tokens * 2 * D, transcendentals=2 * tokens * KEYS
        ),
        name="attention_backward",
    )(queries, keys, values, outputs, dout, lse)
    dq = pltpu.with_memory_space_constraint(dq, pltpu.VMEM)
    return pl.pallas_call(
        finish,
        out_shape=(
            jax.ShapeDtypeStruct(dq.shape, BF16),
            jax.ShapeDtypeStruct(keys.shape, BF16),
            jax.ShapeDtypeStruct(values.shape, BF16),
        ),
        in_specs=[vmem, vmem],
        out_specs=(hbm, vmem, vmem),
        scratch_shapes=[dma((FINISH,))],
        cost_estimate=pl.CostEstimate(flops=0, bytes_accessed=4 * tokens * 2 * D, transcendentals=0),
        name="finish",
    )(dq, terms)


def solution(mesh):
    placed = (
        P("ctx", "head"),
        P(("head", "ctx"), None),
        P(("head", "ctx"), None),
        P("ctx", "head"),
        P(("ctx", "head"), None),
        P("head", "ctx"),
    )
    return jax.shard_map(
        on_device,
        mesh=mesh,
        in_specs=placed,
        out_specs=(P("ctx", "head"), P(("head", "ctx"), None), P(("head", "ctx"), None)),
        check_vma=False,
    )
```

```python
import functools
import math

import jax
import jax.numpy as jnp
from jax import lax
from jax.experimental import pallas as pl
from jax.experimental.pallas import tpu as pltpu
from jax.sharding import PartitionSpec as P

MESH = pl.DeviceIdType.MESH
D = 128
T = 128
NX, NZL, NC, NY, NZH = 4, 4, 2, 4, 2
NZ = NZL * NZH
NH = NX * NZL * NC
KEYS = 1024
GROUP = 16
KB = 256
AHEAD = 12
PACE = (6, 6, 8)
FINISH = 4
C = D ** (-0.5)
LOG2E = math.log2(math.e)
NT = (((1,), (1,)), ((), ()))
F32, BF16 = jnp.float32, jnp.bfloat16


def div(a, n):
    return lax.div(a, jnp.int32(n))


def rem(a, n):
    return lax.rem(a, jnp.int32(n))


def kernel(
    q_hbm, k_ref, v_ref, o_hbm, d_hbm, lse_ref,
    dq_vm, ra_in,
    q_vm, o_vm, d_vm,
    a_out, a_in, kv16, kv, kk, vv, kt,
    acc, rd_in, rc_out, rc_in, tot, rb_out, rb_in, last, ra_out,
    d_send, d_recv, q_sem, o_sem,
    ka_send, ka_recv, kb_send, kb_recv, kc_send, kc_recv, kd_send, kd_recv,
    rd_send, rd_recv, rc_send, rc_recv, rb_send, rb_recv, ra_send, ra_recv,
):
    head, ctx = lax.axis_index("head"), lax.axis_index("ctx")
    x, zl, core = div(head, NZL * NC), rem(div(head, NC), NZL), rem(head, NC)
    y, zh = div(ctx, NZH), rem(ctx, NZH)
    z = zh * NZL + zl
    za, zb = div(zl, 2), rem(zl, 2)

    def device(x_=x, zl_=zl, core_=core, y_=y, zh_=zh):
        return ((x_ * NZL + zl_) * NC + core_, y_ * NZH + zh_)

    def partner(j, way):
        da, dx, dc, db = rem(j, 2), rem(div(j, 2), NX), rem(div(j, 2 * NX), 2), div(j, 4 * NX)
        core_ = rem(core + dc, NC)
        turn = way * (1 - 2 * (core if way == 1 else core_))
        x_ = rem(x + NX + turn * dx, NX)
        zl_ = rem(za + da, 2) * 2 + rem(zb + db, 2)
        return (x_ * NZL + zl_) * NC + core_

    q_copy = pltpu.make_async_copy(q_hbm, q_vm, q_sem)
    o_copy = pltpu.make_async_copy(o_hbm, o_vm, o_sem)
    own = pltpu.make_async_copy(
        d_hbm.at[:, pl.ds(pl.multiple_of(head * 2 * D, 2 * D), 2 * D)], d_vm.at[head], d_recv.at[0]
    )

    barrier = pltpu.get_barrier_semaphore()

    @pl.loop(1, NH)
    def _(j):
        pl.semaphore_signal(barrier, inc=1, device_id=(partner(j, 1), ctx), device_id_type=MESH)

    for r in range(1, NY):
        pl.semaphore_signal(barrier, inc=1, device_id=device(y_=rem(y + r, NY)), device_id_type=MESH)
    for r in range(NZL):
        pl.semaphore_signal(
            barrier, inc=1, device_id=device(zl_=rem(zl + r, NZL), zh_=1 - zh), device_id_type=MESH
        )
    for g in range(NX):
        a_out[g, 0:4, :] = k_ref[:, g * D : (g + 1) * D].astype(F32)
        a_out[g, 4:8, :] = v_ref[:, g * D : (g + 1) * D].astype(F32)
    pl.semaphore_wait(barrier, NH - 1 + NY - 1 + NZL)

    def exchange(n, me, target, src, dst, send, recv):
        copies = []
        for r in sorted(range(1, n), key=lambda r: -min(r, n - r)):
            to = rem(me + r, n)
            copy = pltpu.make_async_remote_copy(
                src_ref=src(to), dst_ref=dst(me), send_sem=send.at[r], recv_sem=recv.at[r],
                device_id=target(to), device_id_type=MESH,
            )
            copy.start()
            copies.append(copy)
        return copies

    ka = exchange(NX, x, lambda i: device(x_=i), lambda i: a_out.at[i], lambda i: a_in.at[i], ka_send, ka_recv)

    def block_copy(j):
        to = partner(j, 1)
        return pltpu.make_async_remote_copy(
            src_ref=d_hbm.at[:, pl.ds(pl.multiple_of(to * 2 * D, 2 * D), 2 * D)],
            dst_ref=d_vm.at[head],
            send_sem=d_send.at[j], recv_sem=d_recv.at[j],
            device_id=(to, ctx), device_id_type=MESH,
        )

    def start_blocks(first, end):
        @pl.loop(first, end)
        def _(j):
            block_copy(j).start()

    start_blocks(1, 1 + PACE[0])
    a_in[x] = a_out[x]
    for copy in ka:
        copy.wait()
    for p in range(NX):
        kv16[0, 4 * p : 4 * p + 4, :] = a_in[p, 0:4, :]
        kv16[1, 4 * p : 4 * p + 4, :] = a_in[p, 4:8, :]
    kv[core, y, z] = kv16[...].astype(BF16)

    def zdev(i):
        return device(zl_=rem(i, NZL), zh_=div(i, NZL))

    kb = exchange(NZ, z, zdev, lambda i: kv.at[core, y, z], lambda i: kv.at[core, y, i], kb_send, kb_recv)
    start_blocks(1 + PACE[0], 1 + PACE[0] + PACE[1])
    own.start()
    q_copy.start()
    o_copy.start()
    acc[...] = jnp.zeros_like(acc)
    for copy in kb:
        copy.wait()
    kc = exchange(NY, y, lambda i: device(y_=i), lambda i: kv.at[core, y], lambda i: kv.at[core, i], kc_send, kc_recv)

    def sibling(r):
        at = rem(y + NY - r, NY)
        return pltpu.make_async_remote_copy(
            src_ref=kv.at[core, at], dst_ref=kv.at[core, at], send_sem=kd_send.at[r], recv_sem=kd_recv.at[r],
            device_id=device(core_=1 - core), device_id_type=MESH,
        )

    sibling(0).start()
    start_blocks(1 + PACE[0] + PACE[1], 1 + sum(PACE))
    for i, r in enumerate((2, 1, 3)):
        kc[i].wait()
        sibling(r).start()
    for r in range(NY):
        sibling(r).wait()
    for i in range(NC * NY):
        rows = slice(i * 128, (i + 1) * 128)
        kk[rows, :] = kv[i // NY, i % NY, :, 0].reshape(128, D)
        vv[rows, :] = kv[i // NY, i % NY, :, 1].reshape(128, D)
    for i in range(KEYS // KB):
        kt[:, i * KB : (i + 1) * KB] = kk[i * KB : (i + 1) * KB, :].T
    q_copy.wait()
    o_copy.wait()

    def stack(block):
        return jnp.concatenate([block[:, :D], block[:, D:]], axis=0)

    def arrived(j):
        src = partner(j, -1)
        pltpu.make_async_copy(d_vm.at[src], d_vm.at[src], d_recv.at[j]).wait()
        return src

    @pl.loop(0, NH, step=2)
    def _(j):
        for i in range(2):
            ahead = AHEAD + j + i

            @pl.when((ahead > sum(PACE)) & (ahead < NH))
            def _():
                block_copy(ahead).start()

        pair = [arrived(j), arrived(j + 1)]
        rows = [pl.ds(pl.multiple_of(src * T, T), T) for src in pair]
        q = jnp.concatenate([stack(q_vm[at, :]) for at in rows], axis=0)
        d = jnp.concatenate([stack(d_vm[src]) for src in pair], axis=0)
        o = jnp.concatenate([stack(o_vm[at, :]) for at in rows], axis=0)
        delta = jnp.sum((d.astype(F32) * o.astype(F32)).T, axis=0, keepdims=True)
        lse = [lse_ref[:, at] * LOG2E for at in rows]
        lse = jnp.concatenate([row for pairs in lse for row in (pairs[0:1], pairs[1:2])], axis=1)
        dqt = jnp.zeros((D, 4 * T), F32)
        for i in range(KEYS // KB):
            at = slice(i * KB, (i + 1) * KB)
            s = lax.dot_general(kk[at, :], q, NT, preferred_element_type=F32)
            p = jnp.exp2(s * (C * LOG2E) - lse)
            dp = lax.dot_general(vv[at, :], d, NT, preferred_element_type=F32)
            ds = (p * (dp - delta)).astype(BF16)
            acc[1, at, :] += jnp.dot(p.astype(BF16), d, preferred_element_type=F32)
            acc[0, at, :] += jnp.dot(ds, q, preferred_element_type=F32)
            dqt = dqt + jnp.dot(kt[:, at], ds, preferred_element_type=F32)
        dq = (dqt * C).T.astype(BF16)
        for i in range(2):
            dq_vm[rows[i], 0:D] = dq[2 * i * T : (2 * i + 1) * T]
            dq_vm[rows[i], D : 2 * D] = dq[(2 * i + 1) * T : (2 * i + 2) * T]

    half = KEYS // NC
    part = half // NY
    rd = []
    for r in (2, 1, 3, 0):
        to = rem(y + r, NY)
        copy = pltpu.make_async_remote_copy(
            src_ref=acc.at[:, pl.ds(pl.multiple_of((1 - core) * half + to * part, part), part), :],
            dst_ref=rd_in.at[to], send_sem=rd_send.at[r], recv_sem=rd_recv.at[r],
            device_id=device(core_=1 - core), device_id_type=MESH,
        )
        copy.start()
        rd.append(copy)

    def both(yy):
        return acc[:, pl.ds(pl.multiple_of(core * half + yy * part, part), part), :] + rd_in[yy]

    rc = []
    for i, r in enumerate((2, 1, 3)):
        to = rem(y + r, NY)
        rd[i].wait_recv()
        rc_out[to] = both(to).astype(rc_out.dtype)
        copy = pltpu.make_async_remote_copy(
            src_ref=rc_out.at[to], dst_ref=rc_in.at[y], send_sem=rc_send.at[r], recv_sem=rc_recv.at[r],
            device_id=device(y_=to), device_id_type=MESH,
        )
        copy.start()
        rc.append(copy)
    rd[NY - 1].wait_recv()
    tot[...] = both(y)
    for i, r in enumerate((2, 1, 3)):
        rc[i].wait_recv()
        tot[...] += rc_in[rem(y + NY - r, NY)].astype(F32)
    for zz in range(NZ):
        rb_out[zz] = tot[:, zz * GROUP : (zz + 1) * GROUP, :].astype(rb_out.dtype)
    rb = exchange(NZ, z, zdev, lambda i: rb_out.at[i], lambda i: rb_in.at[i], rb_send, rb_recv)
    last[...] = tot[:, pl.ds(pl.multiple_of(z * GROUP, GROUP), GROUP), :]
    for copy in rb:
        copy.wait_recv()
    terms = last[...]
    for r in range(1, NZ):
        terms = terms + rb_in[rem(z + NZ - r, NZ)].astype(F32)
    last[...] = terms
    for p in range(NX):
        ra_out[p, 0:4, :] = last[0, 4 * p : 4 * p + 4, :] * C
        ra_out[p, 4:8, :] = last[1, 4 * p : 4 * p + 4, :]
    ra = exchange(NX, x, lambda i: device(x_=i), lambda i: ra_out.at[i], lambda i: ra_in.at[i], ra_send, ra_recv)
    ra_in[x] = ra_out[x]

    @pl.loop(1, NH)
    def _(j):
        block_copy(j).wait_send()

    for copy in rd + rc + rb:
        copy.wait_send()
    for copy in ra:
        copy.wait()


def finish(dq_in, terms, dq_hbm, dk_hbm, dv_hbm, low, sem):
    rows = dq_in.shape[0] // FINISH
    copies = [
        pltpu.make_async_copy(dq_in.at[i * rows : (i + 1) * rows], dq_hbm.at[i * rows : (i + 1) * rows], sem.at[i])
        for i in range(FINISH)
    ]
    for copy in copies:
        copy.start()
    for i, out in enumerate((dk_hbm, dv_hbm)):
        for g in range(NX):
            low[i, :, g * D : (g + 1) * D] = terms[g, 4 * i : 4 * i + 4, :].astype(BF16)
        copy = pltpu.make_async_copy(low.at[i], out, sem.at[FINISH + i])
        copy.start()
        copies.append(copy)
    for copy in copies:
        copy.wait()


def on_device(queries, keys, values, outputs, dout, lse):
    tokens = queries.shape[0]
    wire = BF16
    dma = pltpu.SemaphoreType.DMA
    part = KEYS // NC // NY
    hbm = pl.BlockSpec(memory_space=pltpu.HBM)
    vmem = pl.BlockSpec(memory_space=pltpu.VMEM)
    flops = 5 * 2 * 2 * tokens * KEYS * D
    dq, terms = pl.pallas_call(
        kernel,
        out_shape=(
            pltpu.VMEM((tokens, 2 * D), BF16),
            pltpu.VMEM((NX, 8, D), F32),
        ),
        in_specs=[hbm, vmem, vmem, hbm, hbm, vmem],
        out_specs=(vmem, vmem),
        scratch_shapes=[
            pltpu.VMEM((tokens, 2 * D), BF16),
            pltpu.VMEM((tokens, 2 * D), BF16),
            pltpu.VMEM((NH, T, 2 * D), BF16),
            pltpu.VMEM((NX, 8, D), F32),
            pltpu.VMEM((NX, 8, D), F32),
            pltpu.VMEM((2, GROUP, D), F32),
            pltpu.VMEM((NC, NY, NZ, 2, GROUP, D), BF16),
            pltpu.VMEM((KEYS, D), BF16),
            pltpu.VMEM((KEYS, D), BF16),
            pltpu.VMEM((D, KEYS), BF16),
            pltpu.VMEM((2, KEYS, D), F32),
            pltpu.VMEM((NY, 2, part, D), F32),
            pltpu.VMEM((NY, 2, part, D), wire),
            pltpu.VMEM((NY, 2, part, D), wire),
            pltpu.VMEM((2, part, D), F32),
            pltpu.VMEM((NZ, 2, GROUP, D), wire),
            pltpu.VMEM((NZ, 2, GROUP, D), wire),
            pltpu.VMEM((2, GROUP, D), F32),
            pltpu.VMEM((NX, 8, D), F32),
            dma((NH,)), dma((NH,)), dma, dma,
            dma((NX,)), dma((NX,)), dma((NZ,)), dma((NZ,)), dma((NY,)), dma((NY,)), dma((NY,)), dma((NY,)),
            dma((NY,)), dma((NY,)), dma((NY,)), dma((NY,)), dma((NZ,)), dma((NZ,)), dma((NX,)), dma((NX,)),
        ],
        compiler_params=pltpu.CompilerParams(
            collective_id=0, has_side_effects=True, vmem_limit_bytes=56 * 1024 * 1024
        ),
        cost_estimate=pl.CostEstimate(
            flops=flops, bytes_accessed=8 * tokens * 2 * D, transcendentals=2 * tokens * KEYS
        ),
        name="attention_backward",
    )(queries, keys, values, outputs, dout, lse)
    dq, terms = (pltpu.with_memory_space_constraint(a, pltpu.VMEM) for a in (dq, terms))
    return pl.pallas_call(
        finish,
        out_shape=(
            jax.ShapeDtypeStruct(dq.shape, BF16),
            jax.ShapeDtypeStruct(keys.shape, BF16),
            jax.ShapeDtypeStruct(values.shape, BF16),
        ),
        in_specs=[vmem, vmem],
        out_specs=(hbm, hbm, hbm),
        scratch_shapes=[pltpu.VMEM((2, *keys.shape), BF16), dma((FINISH + 2,))],
        cost_estimate=pl.CostEstimate(flops=0, bytes_accessed=4 * tokens * 2 * D, transcendentals=0),
        name="finish",
    )(dq, terms)


def solution(mesh):
    placed = (
        P("ctx", "head"),
        P(("head", "ctx"), None),
        P(("head", "ctx"), None),
        P("ctx", "head"),
        P(("ctx", "head"), None),
        P("head", "ctx"),
    )
    return jax.shard_map(
        on_device,
        mesh=mesh,
        in_specs=placed,
        out_specs=(P("ctx", "head"), P(("head", "ctx"), None), P(("head", "ctx"), None)),
        check_vma=False,
    )
```

```python
import functools
import math

import jax
import jax.numpy as jnp
from jax import lax
from jax.experimental import pallas as pl
from jax.experimental.pallas import tpu as pltpu
from jax.sharding import PartitionSpec as P

MESH = pl.DeviceIdType.MESH
D = 128
T = 128
NX, NZL, NC, NY, NZH = 4, 4, 2, 4, 2
NZ = NZL * NZH
NH = NX * NZL * NC
KEYS = 1024
GROUP = 16
KB = 256
AHEAD = 12
PACE = (6, 6, 8)
FINISH = 4
C = D ** (-0.5)
LOG2E = math.log2(math.e)
NT = (((1,), (1,)), ((), ()))
F32, BF16 = jnp.float32, jnp.bfloat16


def div(a, n):
    return lax.div(a, jnp.int32(n))


def rem(a, n):
    return lax.rem(a, jnp.int32(n))


def kernel(
    q_hbm, k_ref, v_ref, o_hbm, d_hbm, lse_ref,
    dq_vm, ra_in,
    q_vm, o_vm, d_vm,
    a_out, a_in, kv16, kv, kk, vv, kt,
    acc, rd_in, rc_out, rc_in, tot, rb_out, rb_in, last, ra_out,
    d_send, d_recv, q_sem, o_sem,
    ka_send, ka_recv, kb_send, kb_recv, kc_send, kc_recv, kd_send, kd_recv,
    rd_send, rd_recv, rc_send, rc_recv, rb_send, rb_recv, ra_send, ra_recv,
):
    head, ctx = lax.axis_index("head"), lax.axis_index("ctx")
    x, zl, core = div(head, NZL * NC), rem(div(head, NC), NZL), rem(head, NC)
    y, zh = div(ctx, NZH), rem(ctx, NZH)
    z = zh * NZL + zl
    za, zb = div(zl, 2), rem(zl, 2)

    def device(x_=x, zl_=zl, core_=core, y_=y, zh_=zh):
        return ((x_ * NZL + zl_) * NC + core_, y_ * NZH + zh_)

    def partner(j, way):
        da, dx, dc, db = rem(j, 2), rem(div(j, 2), NX), rem(div(j, 2 * NX), 2), div(j, 4 * NX)
        core_ = rem(core + dc, NC)
        turn = way * (1 - 2 * (core if way == 1 else core_))
        x_ = rem(x + NX + turn * dx, NX)
        zl_ = rem(za + da, 2) * 2 + rem(zb + db, 2)
        return (x_ * NZL + zl_) * NC + core_

    q_copy = pltpu.make_async_copy(q_hbm, q_vm, q_sem)
    o_copy = pltpu.make_async_copy(o_hbm, o_vm, o_sem)
    own = pltpu.make_async_copy(
        d_hbm.at[:, pl.ds(pl.multiple_of(head * 2 * D, 2 * D), 2 * D)], d_vm.at[head], d_recv.at[0]
    )

    barrier = pltpu.get_barrier_semaphore()

    @pl.loop(1, NH)
    def _(j):
        pl.semaphore_signal(barrier, inc=1, device_id=(partner(j, 1), ctx), device_id_type=MESH)

    for r in range(1, NY):
        pl.semaphore_signal(barrier, inc=1, device_id=device(y_=rem(y + r, NY)), device_id_type=MESH)
    for r in range(NZL):
        pl.semaphore_signal(
            barrier, inc=1, device_id=device(zl_=rem(zl + r, NZL), zh_=1 - zh), device_id_type=MESH
        )
    for g in range(NX):
        a_out[g, 0:4, :] = k_ref[:, g * D : (g + 1) * D].astype(F32)
        a_out[g, 4:8, :] = v_ref[:, g * D : (g + 1) * D].astype(F32)
    pl.semaphore_wait(barrier, NH - 1 + NY - 1 + NZL)

    def exchange(n, me, target, src, dst, send, recv):
        copies = []
        for r in sorted(range(1, n), key=lambda r: -min(r, n - r)):
            to = rem(me + r, n)
            copy = pltpu.make_async_remote_copy(
                src_ref=src(to), dst_ref=dst(me), send_sem=send.at[r], recv_sem=recv.at[r],
                device_id=target(to), device_id_type=MESH,
            )
            copy.start()
            copies.append(copy)
        return copies

    ka = exchange(NX, x, lambda i: device(x_=i), lambda i: a_out.at[i], lambda i: a_in.at[i], ka_send, ka_recv)

    def block_copy(j):
        to = partner(j, 1)
        return pltpu.make_async_remote_copy(
            src_ref=d_hbm.at[:, pl.ds(pl.multiple_of(to * 2 * D, 2 * D), 2 * D)],
            dst_ref=d_vm.at[head],
            send_sem=d_send.at[j], recv_sem=d_recv.at[j],
            device_id=(to, ctx), device_id_type=MESH,
        )

    def start_blocks(first, end):
        @pl.loop(first, end)
        def _(j):
            block_copy(j).start()

    start_blocks(1, 1 + PACE[0])
    a_in[x] = a_out[x]
    for copy in ka:
        copy.wait()
    for p in range(NX):
        kv16[0, 4 * p : 4 * p + 4, :] = a_in[p, 0:4, :]
        kv16[1, 4 * p : 4 * p + 4, :] = a_in[p, 4:8, :]
    kv[core, y, z] = kv16[...].astype(BF16)

    def zdev(i):
        return device(zl_=rem(i, NZL), zh_=div(i, NZL))

    kb = exchange(NZ, z, zdev, lambda i: kv.at[core, y, z], lambda i: kv.at[core, y, i], kb_send, kb_recv)
    start_blocks(1 + PACE[0], 1 + PACE[0] + PACE[1])
    own.start()
    q_copy.start()
    o_copy.start()
    acc[...] = jnp.zeros_like(acc)
    for copy in kb:
        copy.wait()
    kc = exchange(NY, y, lambda i: device(y_=i), lambda i: kv.at[core, y], lambda i: kv.at[core, i], kc_send, kc_recv)

    def sibling(r):
        at = rem(y + NY - r, NY)
        return pltpu.make_async_remote_copy(
            src_ref=kv.at[core, at], dst_ref=kv.at[core, at], send_sem=kd_send.at[r], recv_sem=kd_recv.at[r],
            device_id=device(core_=1 - core), device_id_type=MESH,
        )

    sibling(0).start()
    start_blocks(1 + PACE[0] + PACE[1], 1 + sum(PACE))
    for i, r in enumerate((2, 1, 3)):
        kc[i].wait()
        sibling(r).start()
    for r in range(NY):
        sibling(r).wait()
    for i in range(NC * NY):
        rows = slice(i * 128, (i + 1) * 128)
        kk[rows, :] = kv[i // NY, i % NY, :, 0].reshape(128, D)
        vv[rows, :] = kv[i // NY, i % NY, :, 1].reshape(128, D)
    for i in range(KEYS // KB):
        kt[:, i * KB : (i + 1) * KB] = kk[i * KB : (i + 1) * KB, :].T
    q_copy.wait()
    o_copy.wait()

    def stack(block):
        return jnp.concatenate([block[:, :D], block[:, D:]], axis=0)

    def arrived(j):
        src = partner(j, -1)
        pltpu.make_async_copy(d_vm.at[src], d_vm.at[src], d_recv.at[j]).wait()
        return src

    half = KEYS // NC
    part = half // NY
    rd = []
    for r in (2, 1, 3, 0):
        to = rem(y + r, NY)
        copy = pltpu.make_async_remote_copy(
            src_ref=acc.at[:, pl.ds(pl.multiple_of((1 - core) * half + to * part, part), part), :],
            dst_ref=rd_in.at[to], send_sem=rd_send.at[r], recv_sem=rd_recv.at[r],
            device_id=device(core_=1 - core), device_id_type=MESH,
        )
        rd.append(copy)

    def compute(j, last_pair):
        pair = [arrived(j), arrived(j + 1)]
        rows = [pl.ds(pl.multiple_of(src * T, T), T) for src in pair]
        q = jnp.concatenate([stack(q_vm[at, :]) for at in rows], axis=0)
        d = jnp.concatenate([stack(d_vm[src]) for src in pair], axis=0)
        o = jnp.concatenate([stack(o_vm[at, :]) for at in rows], axis=0)
        delta = jnp.sum((d.astype(F32) * o.astype(F32)).T, axis=0, keepdims=True)
        lse = [lse_ref[:, at] * LOG2E for at in rows]
        lse = jnp.concatenate([row for pairs in lse for row in (pairs[0:1], pairs[1:2])], axis=1)
        dqt = jnp.zeros((D, 4 * T), F32)
        for i in range(KEYS // KB):
            at = pl.ds(i * KB, KB)
            if last_pair:
                turn = rem((1 - core) * (half // KB) + i, KEYS // KB)
                at = pl.ds(pl.multiple_of(turn * KB, KB), KB)
            s = lax.dot_general(kk[at, :], q, NT, preferred_element_type=F32)
            p = jnp.exp2(s * (C * LOG2E) - lse)
            dp = lax.dot_general(vv[at, :], d, NT, preferred_element_type=F32)
            ds = (p * (dp - delta)).astype(BF16)
            acc[1, at, :] += jnp.dot(p.astype(BF16), d, preferred_element_type=F32)
            acc[0, at, :] += jnp.dot(ds, q, preferred_element_type=F32)
            dqt = dqt + jnp.dot(kt[:, at], ds, preferred_element_type=F32)
            if last_pair and (i + 1) * KB == half:
                for copy in rd:
                    copy.start()
        dq = (dqt * C).T.astype(BF16)
        for i in range(2):
            dq_vm[rows[i], 0:D] = dq[2 * i * T : (2 * i + 1) * T]
            dq_vm[rows[i], D : 2 * D] = dq[(2 * i + 1) * T : (2 * i + 2) * T]

    @pl.loop(0, NH - 2, step=2)
    def _(j):
        for i in range(2):
            ahead = AHEAD + j + i

            @pl.when((ahead > sum(PACE)) & (ahead < NH))
            def _():
                block_copy(ahead).start()

        compute(j, False)

    compute(jnp.int32(NH - 2), True)

    def both(yy):
        return acc[:, pl.ds(pl.multiple_of(core * half + yy * part, part), part), :] + rd_in[yy]

    rc = []
    for i, r in enumerate((2, 1, 3)):
        to = rem(y + r, NY)
        rd[i].wait_recv()
        rc_out[to] = both(to).astype(rc_out.dtype)
        copy = pltpu.make_async_remote_copy(
            src_ref=rc_out.at[to], dst_ref=rc_in.at[y], send_sem=rc_send.at[r], recv_sem=rc_recv.at[r],
            device_id=device(y_=to), device_id_type=MESH,
        )
        copy.start()
        rc.append(copy)
    rd[NY - 1].wait_recv()
    tot[...] = both(y)
    for i, r in enumerate((2, 1, 3)):
        rc[i].wait_recv()
        tot[...] += rc_in[rem(y + NY - r, NY)].astype(F32)
    for zz in range(NZ):
        rb_out[zz] = tot[:, zz * GROUP : (zz + 1) * GROUP, :].astype(rb_out.dtype)
    rb = exchange(NZ, z, zdev, lambda i: rb_out.at[i], lambda i: rb_in.at[i], rb_send, rb_recv)
    last[...] = tot[:, pl.ds(pl.multiple_of(z * GROUP, GROUP), GROUP), :]
    for copy in rb:
        copy.wait_recv()
    terms = last[...]
    for r in range(1, NZ):
        terms = terms + rb_in[rem(z + NZ - r, NZ)].astype(F32)
    last[...] = terms
    for p in range(NX):
        ra_out[p, 0:4, :] = last[0, 4 * p : 4 * p + 4, :] * C
        ra_out[p, 4:8, :] = last[1, 4 * p : 4 * p + 4, :]
    ra = exchange(NX, x, lambda i: device(x_=i), lambda i: ra_out.at[i], lambda i: ra_in.at[i], ra_send, ra_recv)
    ra_in[x] = ra_out[x]

    @pl.loop(1, NH)
    def _(j):
        block_copy(j).wait_send()

    for copy in rd + rc + rb:
        copy.wait_send()
    for copy in ra:
        copy.wait()


def finish(dq_in, terms, dq_hbm, dk_hbm, dv_hbm, low, sem):
    rows = dq_in.shape[0] // FINISH
    copies = [
        pltpu.make_async_copy(dq_in.at[i * rows : (i + 1) * rows], dq_hbm.at[i * rows : (i + 1) * rows], sem.at[i])
        for i in range(FINISH)
    ]
    for copy in copies:
        copy.start()
    for i, out in enumerate((dk_hbm, dv_hbm)):
        for g in range(NX):
            low[i, :, g * D : (g + 1) * D] = terms[g, 4 * i : 4 * i + 4, :].astype(BF16)
        copy = pltpu.make_async_copy(low.at[i], out, sem.at[FINISH + i])
        copy.start()
        copies.append(copy)
    for copy in copies:
        copy.wait()


def on_device(queries, keys, values, outputs, dout, lse):
    tokens = queries.shape[0]
    wire = BF16
    dma = pltpu.SemaphoreType.DMA
    part = KEYS // NC // NY
    hbm = pl.BlockSpec(memory_space=pltpu.HBM)
    vmem = pl.BlockSpec(memory_space=pltpu.VMEM)
    flops = 5 * 2 * 2 * tokens * KEYS * D
    dq, terms = pl.pallas_call(
        kernel,
        out_shape=(
            pltpu.VMEM((tokens, 2 * D), BF16),
            pltpu.VMEM((NX, 8, D), F32),
        ),
        in_specs=[hbm, vmem, vmem, hbm, hbm, vmem],
        out_specs=(vmem, vmem),
        scratch_shapes=[
            pltpu.VMEM((tokens, 2 * D), BF16),
            pltpu.VMEM((tokens, 2 * D), BF16),
            pltpu.VMEM((NH, T, 2 * D), BF16),
            pltpu.VMEM((NX, 8, D), F32),
            pltpu.VMEM((NX, 8, D), F32),
            pltpu.VMEM((2, GROUP, D), F32),
            pltpu.VMEM((NC, NY, NZ, 2, GROUP, D), BF16),
            pltpu.VMEM((KEYS, D), BF16),
            pltpu.VMEM((KEYS, D), BF16),
            pltpu.VMEM((D, KEYS), BF16),
            pltpu.VMEM((2, KEYS, D), F32),
            pltpu.VMEM((NY, 2, part, D), F32),
            pltpu.VMEM((NY, 2, part, D), wire),
            pltpu.VMEM((NY, 2, part, D), wire),
            pltpu.VMEM((2, part, D), F32),
            pltpu.VMEM((NZ, 2, GROUP, D), wire),
            pltpu.VMEM((NZ, 2, GROUP, D), wire),
            pltpu.VMEM((2, GROUP, D), F32),
            pltpu.VMEM((NX, 8, D), F32),
            dma((NH,)), dma((NH,)), dma, dma,
            dma((NX,)), dma((NX,)), dma((NZ,)), dma((NZ,)), dma((NY,)), dma((NY,)), dma((NY,)), dma((NY,)),
            dma((NY,)), dma((NY,)), dma((NY,)), dma((NY,)), dma((NZ,)), dma((NZ,)), dma((NX,)), dma((NX,)),
        ],
        compiler_params=pltpu.CompilerParams(
            collective_id=0, has_side_effects=True, vmem_limit_bytes=56 * 1024 * 1024
        ),
        cost_estimate=pl.CostEstimate(
            flops=flops, bytes_accessed=8 * tokens * 2 * D, transcendentals=2 * tokens * KEYS
        ),
        name="attention_backward",
    )(queries, keys, values, outputs, dout, lse)
    dq, terms = (pltpu.with_memory_space_constraint(a, pltpu.VMEM) for a in (dq, terms))
    return pl.pallas_call(
        finish,
        out_shape=(
            jax.ShapeDtypeStruct(dq.shape, BF16),
            jax.ShapeDtypeStruct(keys.shape, BF16),
            jax.ShapeDtypeStruct(values.shape, BF16),
        ),
        in_specs=[vmem, vmem],
        out_specs=(hbm, hbm, hbm),
        scratch_shapes=[pltpu.VMEM((2, *keys.shape), BF16), dma((FINISH + 2,))],
        cost_estimate=pl.CostEstimate(flops=0, bytes_accessed=4 * tokens * 2 * D, transcendentals=0),
        name="finish",
    )(dq, terms)


def solution(mesh):
    placed = (
        P("ctx", "head"),
        P(("head", "ctx"), None),
        P(("head", "ctx"), None),
        P("ctx", "head"),
        P(("ctx", "head"), None),
        P("head", "ctx"),
    )
    return jax.shard_map(
        on_device,
        mesh=mesh,
        in_specs=placed,
        out_specs=(P("ctx", "head"), P(("head", "ctx"), None), P(("head", "ctx"), None)),
        check_vma=False,
    )
```
